128 devices in a mesh: front: 32 (over z, y, x_lo), row: 2 (over core), col: 2 (over x_hi).
Axes of the slice: x: 4 (x_hi: 2, x_lo: 2; x = x_hi * 2 + x_lo), y: 4, z: 4, core: 2. Of those that a mesh axis runs over, the one named last changes fastest.
Arguments:
- front: bfloat16 [32, 4096, 4096], P('front', 'row', 'col'), may hold values from -6 to 30
- inverses: bfloat16 [32, 2, 256, 256], P('front'), may hold values from -0.2 to 0.2
- routes: int32 [32, 16, 16], P('front', 'row', 'col'), may hold values from -1 to 31, as said below
- positions: int32 [32, 16, 16], P('front', 'row', 'col'), may hold values from 0 to 63
- parent: bfloat16 [32, 4096, 4096], P('front', 'row', 'col'), may hold values from -6 to 6
Outputs:
- factor: bfloat16 [32, 4096, 512], P('front', 'row', 'col')
- parent_out: bfloat16 [32, 4096, 4096], P('front', 'row', 'col')
The draws below stay inside these ranges and needn't reach their ends.
Inputs may be any that keep to these rules, and one draw needn't show every extreme that they name: `routes`: -1 exactly on blocks whose block row or block column is under 2; at most 2 blocks held by one device name one group, and in every draw some group is named by exactly 2 blocks of every device of some grid position. `positions`: a block of the receiving device's share of the parent front, counted row by row.
All inputs are finite; a program needn't handle non-finite values.
Results may differ from the reference program's by a relative error of at most 0.0055.
Values may be sent and summed in bfloat16 or wider, within the bound.
A program may use at most 192 MiB of HBM per device.

```python
import jax
import jax.numpy as jnp
from jax import lax

F = 4096
NB = 256
PANELS = 2
NBLK = 16
TILES_DEV = 64
N_FRONT = 32
N_ROW = 2
N_COL = 2


def draw_front(key, part):
    key = jax.random.fold_in(key, 1)
    noise = jnp.clip(jax.random.normal(key, (N_FRONT, F, F), jnp.float32), -4.0, 4.0)
    matrix = (noise + jnp.swapaxes(noise, 1, 2)) * 0.7071
    matrix = matrix + 24.0 * jnp.eye(F, dtype=jnp.float32)[None]
    return matrix.astype(jnp.bfloat16)


def draw_inverses(key, part):
    key = jax.random.fold_in(key, 2)
    noise_key, diag_key = jax.random.split(key)
    noise = jnp.clip(jax.random.normal(noise_key, (N_FRONT, PANELS, NB, NB), jnp.float32), -4.0, 4.0)
    noise = noise * (0.5 / NB ** 0.5)
    diag = jax.random.uniform(diag_key, (N_FRONT, PANELS, NB), jnp.float32, 0.6, 1.4)
    inverse = (jnp.eye(NB, dtype=jnp.float32) * diag[..., None] + noise) / 24.0
    return inverse.astype(jnp.bfloat16)


def draw_routes(key, part):
    key = jax.random.fold_in(key, 3)
    score_key, favour_key = jax.random.split(key)
    row_blocks = F // N_ROW // NB
    col_blocks = F // N_COL // NB
    tile_count = row_blocks * col_blocks
    groups = jnp.arange(N_FRONT, dtype=jnp.int32)
    scores = jax.random.randint(score_key, (N_FRONT, N_ROW, N_COL, N_FRONT), 0, 2 ** 20) * N_FRONT + groups
    favour = jax.random.randint(favour_key, (N_ROW, N_COL), 0, N_FRONT)
    scores = jnp.where(groups == favour[None, :, :, None], -1, scores)
    order = jnp.argsort(scores, axis=-1, stable=True).astype(jnp.int32)
    block_rows = jnp.arange(N_ROW)[:, None, None, None] * row_blocks + jnp.arange(row_blocks)[None, None, :, None]
    block_cols = jnp.arange(N_COL)[None, :, None, None] * col_blocks + jnp.arange(col_blocks)[None, None, None, :]
    valid = (block_rows >= PANELS) & (block_cols >= PANELS)
    valid = valid.reshape(N_ROW, N_COL, tile_count)
    rank = jnp.cumsum(valid.astype(jnp.int32), axis=-1) - 1
    pick = jnp.broadcast_to(jnp.maximum(rank, 0) % N_FRONT, (N_FRONT, N_ROW, N_COL, tile_count))
    dest = jnp.take_along_axis(order, pick, axis=-1)
    routed = jnp.where(valid[None], dest, -1).astype(jnp.int32)
    routed = routed.reshape(N_FRONT, N_ROW, N_COL, row_blocks, col_blocks).transpose(0, 1, 3, 2, 4)
    return routed.reshape(N_FRONT, F // NB, F // NB)


def touch_ends(values, rng, low, top_value):
    index_at = [jax.random.randint(jax.random.fold_in(rng, axis), (), 0, length) for axis, length in enumerate(values.shape)]
    main_axis = values.shape.index(max(values.shape))
    next_to = index_at[:main_axis] + [(index_at[main_axis] + 1) % values.shape[main_axis]] + index_at[main_axis + 1:]
    return values.at[tuple(index_at)].set(low).at[tuple(next_to)].set(top_value)


def steps_of(own_key, extent, pieces, low, high):
    def one(axis_at, blocks):
        heights = jax.random.uniform(jax.random.fold_in(jax.random.fold_in(own_key, 6), axis_at), (blocks,), jnp.float32, low / len(pieces), high / len(pieces))
        return jnp.repeat(jnp.exp(heights), extent[axis_at] // blocks).reshape((-1,) + (1,) * (len(extent) - axis_at - 1))

    level = one(*pieces[0])
    for cut in pieces[1:]:
        level = level * one(*cut)
    return level


def gaussian(own_key, dims, deviation, reach, shards=(), held_as=jnp.bfloat16):
    entries = jax.random.normal(own_key, dims, jnp.float32) * deviation
    if len(shards) > 0:
        entries = steps_of(own_key, dims, shards, -0.22, 0.18) * entries
    return jnp.clip(entries, min=-reach, max=reach).astype(held_as)


def setup_inputs(seed: int = 0) -> dict:
    key_list = jax.random.split(jax.random.key(seed), 6)
    return {
        "front": draw_front(jax.random.fold_in(key_list[5], 71), 0),
        "inverses": draw_inverses(jax.random.fold_in(key_list[5], 71), 0),
        "routes": draw_routes(jax.random.fold_in(key_list[5], 71), 0),
        "positions": touch_ends(jax.random.randint(key_list[3], (N_FRONT, NBLK, NBLK), 0, TILES_DEV), jax.random.fold_in(key_list[3], 1), 0, TILES_DEV - 1).astype(jnp.int32),
        "parent": gaussian(key_list[4], (N_FRONT, F, F), 1.0, 6.0, ((0, 32), (1, 2), (2, 2))),
    }


def eliminate(matrix, inverse):
    work = matrix.astype(jnp.float32)
    factors = []
    all_rows = jnp.arange(F)[:, None]
    for panel in range(PANELS):
        lower = panel * NB
        column = work[:, lower:lower + NB].astype(jnp.bfloat16)
        block_row = work[lower:lower + NB, :].astype(jnp.bfloat16)
        product = jnp.dot(column, inverse[panel], preferred_element_type=jnp.float32)
        panel_factor = jnp.where(all_rows >= lower, product, jnp.float32(0.0)).astype(jnp.bfloat16)
        work = work - jnp.dot(panel_factor, block_row, preferred_element_type=jnp.float32)
        factors.append(panel_factor)
    return jnp.concatenate(factors, axis=1), work


def reference(front, inverses, routes, positions, parent):
    row_blocks = F // N_ROW // NB
    col_blocks = F // N_COL // NB
    blocks = F // NB
    block_i = jnp.broadcast_to(jnp.arange(blocks, dtype=jnp.int32)[:, None], (blocks, blocks))
    block_j = jnp.broadcast_to(jnp.arange(blocks, dtype=jnp.int32)[None, :], (blocks, blocks))

    def one_front(totals, inputs):
        matrix, inverse, route, place = inputs
        factor, work = eliminate(matrix, inverse)
        tiles = work.reshape(blocks, NB, blocks, NB).transpose(0, 2, 1, 3)
        valid = route >= 0
        target = jnp.where(valid, route, 0).astype(jnp.int32)
        to_row = ((block_i // row_blocks) * row_blocks + place // col_blocks).astype(jnp.int32)
        to_col = ((block_j // col_blocks) * col_blocks + place % col_blocks).astype(jnp.int32)
        masked = jnp.where(valid[:, :, None, None], tiles, jnp.float32(0.0))
        totals = totals.at[target, to_row, to_col].add(masked)
        return totals, factor

    start = jnp.zeros((N_FRONT, blocks, blocks, NB, NB), jnp.float32)
    totals, factors = lax.scan(one_front, start, (front, inverses, routes, positions))
    added = totals.transpose(0, 1, 3, 2, 4).reshape(N_FRONT, F, F)
    parent_out = (parent.astype(jnp.float32) + added).astype(jnp.bfloat16)
    return factors, parent_out
```

```python
import functools

import jax
import jax.numpy as jnp
from jax import lax
from jax.experimental import pallas as pl
from jax.experimental.pallas import tpu as pltpu
from jax.sharding import PartitionSpec as P

MESH = pl.DeviceIdType.MESH
NB = 256
SIDE = 8
TILES = SIDE * SIDE
GROUPS = 32
WIDTH = SIDE * NB
CHUNKS = (64, 64, 64, 64)
STARTS = tuple(sum(CHUNKS[:q]) for q in range(len(CHUNKS)))
NQ = len(CHUNKS)
F32 = jnp.float32
BF16 = jnp.bfloat16


def hops(d):
    return min(d[0], 4 - d[0]) + min(d[1], 4 - d[1]) + d[2]


OFFSETS = [(z, y, x) for z in range(4) for y in range(4) for x in range(2)]
ORDER = sorted(OFFSETS[1:], key=lambda d: -hops(d))


def dot(a, b):
    return jnp.dot(a, b, preferred_element_type=F32)


def kernel(front, inv, routes, places, parent, fac_out, out, *refs):
    refs = list(refs)

    def take(n):
        got = refs[:n]
        del refs[:n]
        return got

    c_bufs, a_bufs, p_bufs, f_bufs, s_bufs, r_bufs = (take(NQ) for _ in range(6))
    (b_buf, dt, l_buf, tiles, acc, pos_send, pos_recv, tab_v, tab_s, got_v, got_s) = take(11)
    (c_ss, c_rs, a_sem, p_sem, f_sem, o_sem, x_ss, x_rs, pos_ss, pos_rs) = take(10)
    (b_ss, b_rs, dt_ss, dt_rs, t_sem) = take(5)

    me = lax.axis_index("front")
    r = lax.axis_index("row")
    c = lax.axis_index("col")
    z, y, x = me // 8, (me // 2) % 4, me % 2
    sign = jnp.where(r == 0, 1, 3)

    def peer(d):
        return ((z + sign * d[0]) % 4) * 8 + ((y + sign * d[1]) % 4) * 2 + (x + d[2]) % 2

    def rows(q):
        return pl.ds(STARTS[q], CHUNKS[q])

    a_cps = [
        pltpu.make_async_copy(front.at[:, rows(q), :], a_bufs[q], a_sem.at[q]) for q in range(NQ)
    ]
    p_cps = [
        pltpu.make_async_copy(parent.at[:, rows(q), :], p_bufs[q], p_sem.at[q]) for q in range(NQ)
    ]
    c_loc = [
        pltpu.make_async_copy(front.at[:, rows(q), pl.ds(0, 2 * NB)], c_bufs[q], c_rs.at[q])
        for q in range(NQ)
    ]
    b_loc = pltpu.make_async_copy(front.at[pl.ds(0, 2)], b_buf, b_rs)

    @pl.when(r == 0)
    def _():
        b_loc.start()

    @pl.when(c == 0)
    def _():
        for cp in c_loc:
            cp.start()

    for cp in a_cps:
        cp.start()

    bar = pltpu.get_barrier_semaphore()

    def greet(k, _):
        pl.semaphore_signal(
            bar, 1, device_id=((me + k) % GROUPS, r, c), device_id_type=MESH
        )
        return 0

    lax.fori_loop(1, GROUPS, greet, 0)
    pl.semaphore_signal(bar, 1, device_id=(me, 1 - r, c), device_id_type=MESH)
    pl.semaphore_signal(bar, 1, device_id=(me, r, 1 - c), device_id_type=MESH)
    pl.semaphore_signal(bar, 1, device_id=(me, 1 - r, 1 - c), device_id_type=MESH)
    pl.semaphore_wait(bar, GROUPS + 2)

    def dt_copy(i, row):
        if i == 0:
            src = front.at[0, :, pl.ds(NB, NB)]
        else:
            src = front.at[1, :, pl.ds(0, NB)]
        return pltpu.make_async_remote_copy(
            src, dt.at[i], dt_ss.at[i, row], dt_rs.at[i], device_id=(me, row, 1), device_id_type=MESH
        )

    def c_copy(q, low):
        return pltpu.make_async_remote_copy(
            front.at[pl.ds(low, SIDE - low), rows(q), pl.ds(0, 2 * NB)],
            c_bufs[q].at[pl.ds(low, SIDE - low)],
            c_ss.at[q],
            c_rs.at[q],
            device_id=(me, r, 1),
            device_id_type=MESH,
        )

    b_copy = pltpu.make_async_remote_copy(
        front.at[pl.ds(0, 2)], b_buf, b_ss, b_rs, device_id=(me, 1, c), device_id_type=MESH
    )

    @pl.when((r == 0) & (c == 0))
    def _():
        for row in range(2):
            for i in range(2):
                dt_copy(i, row).start()

    @pl.when(r == 0)
    def _():
        b_copy.start()

    for row in range(2):

        @pl.when((r == row) & (c == 0))
        def _():
            for q in range(NQ):
                c_copy(q, 1 - row).start()

    for cp in p_cps:
        cp.start()

    @pl.when((r == 0) & (c == 1))
    def _():
        for q in range(NQ):
            c_bufs[q][0] = jnp.zeros((CHUNKS[q], 2 * NB), BF16)

    lane = lax.broadcasted_iota(jnp.int32, (TILES, 128), 1)
    sub = lax.broadcasted_iota(jnp.int32, (TILES, 128), 0)
    lane1 = lax.broadcasted_iota(jnp.int32, (1, 128), 1)

    def spread(t, carry):
        across, down, place = carry
        route = routes[t // SIDE, t % SIDE]
        across = jnp.where(lane1 == t, route, across)
        down = jnp.where(sub == t, route, down)
        place = jnp.where(lane1 == t, places[t // SIDE, t % SIDE], place)
        return across, down, place

    none1 = jnp.full((1, 128), -1, jnp.int32)
    across, down, place = lax.fori_loop(
        0, TILES, spread, (none1, jnp.full((TILES, 128), -1, jnp.int32), none1)
    )
    same = down == across
    before = jnp.sum(jnp.where(same & (sub < lane), 1, 0), axis=0, keepdims=True)
    slot8 = jnp.where((across >= 0) & (before < 2), across * 8 + before, -1)
    sub8 = lax.broadcasted_iota(jnp.int32, (GROUPS * 8, 128), 0)
    pos = jnp.max(jnp.where(slot8 == sub8, place, -1), axis=1, keepdims=True)
    pos_send[...] = jnp.broadcast_to(pos, (GROUPS * 8, 128))
    before = jnp.sum(jnp.where(same & (lane < sub), 1, 0), axis=1, keepdims=True)
    slot2 = jnp.where(down >= 0, down * 2 + before, -1)
    tab_v[...] = jnp.broadcast_to(
        jnp.max(jnp.where(slot2 == lane, sub, 0), axis=0, keepdims=True), (8, 128)
    )
    tab_cp = pltpu.make_async_copy(tab_v, tab_s, t_sem.at[0])
    tab_cp.start()
    pos_recv[pl.ds(0, 8), :] = pos_send[pl.ds(pl.multiple_of(me * 8, 8), 8), :]

    def pos_copy(d):
        k = OFFSETS.index(d)
        g = peer(d)
        return pltpu.make_async_remote_copy(
            pos_send.at[pl.ds(pl.multiple_of(g * 8, 8), 8)],
            pos_recv.at[pl.ds(8 * k, 8)],
            pos_ss.at[k],
            pos_rs.at[k],
            device_id=(g, r, c),
            device_id_type=MESH,
        )

    for d in ORDER:
        pos_copy(d).start()

    @pl.when(r == 0)
    def _():
        b_loc.wait()

    @pl.when(r == 1)
    def _():
        b_copy.wait_recv()

    @pl.when(c == 0)
    def _():
        dt[0] = b_buf[0, :, pl.ds(NB, NB)]
        dt[1] = b_buf[1, :, pl.ds(0, NB)]

    @pl.when(c == 1)
    def _():
        for i in range(2):
            dt_copy(i, 0).wait_recv()

    panel_d = dot(dt[1], inv[0]).astype(BF16)

    def row_step(j, _):
        cols = pl.ds(pl.multiple_of(j * NB, NB), NB)
        b_buf[1, :, cols] = (
            b_buf[1, :, cols].astype(F32) - dot(panel_d, b_buf[0, :, cols])
        ).astype(BF16)
        return 0

    lax.fori_loop(0, SIDE, row_step, 0)
    tab_cp.wait()

    def x_copy(q, d):
        k = OFFSETS.index(d)
        return pltpu.make_async_remote_copy(
            s_bufs[q].at[pl.ds(2 * k, 2)],
            r_bufs[q].at[pl.ds(2 * k, 2)],
            x_ss.at[q, k],
            x_rs.at[q, k],
            device_id=(peer(d), r, c),
            device_id_type=MESH,
        )

    f_cps = []
    for q in range(NQ):
        size = CHUNKS[q]

        @pl.when(c == 0)
        def _():
            c_loc[q].wait()

        for row in range(2):

            @pl.when((r == row) & (c == 1))
            def _():
                c_copy(q, 1 - row).wait_recv()

        first = c_bufs[q][:, :, pl.ds(0, NB)].reshape(SIDE * size, NB)
        second = c_bufs[q][:, :, pl.ds(NB, NB)].reshape(SIDE * size, NB)
        panel0 = dot(first, inv[0]).astype(BF16)
        second = (second.astype(F32) - dot(panel0, dt[0])).astype(BF16)
        panel1 = dot(second, inv[1])
        line = lax.broadcasted_iota(jnp.int32, panel1.shape, 0)
        panel1 = jnp.where((line < size) & (r == 0), 0.0, panel1).astype(BF16)
        l_buf[pl.ds(0, SIDE * size), pl.ds(0, NB)] = panel0
        l_buf[pl.ds(0, SIDE * size), pl.ds(NB, NB)] = panel1

        @pl.when(c == 0)
        def _():
            f_bufs[q][...] = panel0.reshape(SIDE, size, NB)

        @pl.when(c == 1)
        def _():
            f_bufs[q][...] = panel1.reshape(SIDE, size, NB)

        f_cp = pltpu.make_async_copy(f_bufs[q], fac_out.at[:, rows(q), :], f_sem.at[q])
        f_cp.start()
        f_cps.append(f_cp)
        a_cps[q].wait()

        def tile_step(j, _):
            cols = pl.ds(pl.multiple_of(j * NB, NB), NB)
            both = b_buf[:, :, cols].reshape(2 * NB, NB)
            prod = dot(l_buf[pl.ds(0, SIDE * size), :], both)
            block = a_bufs[q][:, :, cols].astype(F32).reshape(SIDE * size, NB)
            block = (block - prod).astype(BF16).reshape(SIDE, size, NB)
            for i in range(SIDE):
                tiles[i * SIDE + j, pl.ds(0, size), :] = block[i]
            return 0

        lax.fori_loop(0, SIDE, tile_step, 0)

        for s in range(2):
            r_bufs[q][s] = tiles[tab_s[0, 2 * me + s], pl.ds(0, size), :]
        for d in ORDER:
            k = OFFSETS.index(d)
            g = peer(d)
            for s in range(2):
                s_bufs[q][2 * k + s] = tiles[tab_s[0, 2 * g + s], pl.ds(0, size), :]
            x_copy(q, d).start()

    for d in ORDER:
        pos_copy(d).wait_recv()
    got = pos_recv[...]
    lane8 = lax.broadcasted_iota(jnp.int32, (GROUPS * 8, 128), 1)

    def slot_of(v):
        return jnp.where(v >= 0, (v >> 3) * 2 + (v & 1), -1)

    last = jnp.max(jnp.where(got == lane8, sub8, -1), axis=0, keepdims=True)
    got_v[pl.ds(0, 8), :] = jnp.broadcast_to(slot_of(last), (8, 128))
    eye = lax.broadcasted_iota(jnp.int32, (128, 128), 0) == lax.broadcasted_iota(
        jnp.int32, (128, 128), 1
    )
    for h in range(2):
        own = jnp.sum(
            jnp.where(eye, got[h * 128 : (h + 1) * 128], 0), axis=0, keepdims=True
        )
        prev = jnp.max(
            jnp.where((got == own) & (sub8 < lane8 + h * 128), sub8, -1), axis=0, keepdims=True
        )
        prev = jnp.where(own >= 0, prev, -1)
        got_v[pl.ds(8 + 8 * h, 8), :] = jnp.broadcast_to(slot_of(prev), (8, 128))
    got_cp = pltpu.make_async_copy(got_v, got_s, t_sem.at[1])
    got_cp.start()
    got_cp.wait()

    o_cps = []
    for q in range(NQ):
        size = CHUNKS[q]
        for d in ORDER:
            x_copy(q, d).wait_recv()

        def add_step(i, _):
            j = (i // 2) * 8 + i % 2
            prev = got_s[8 + 8 * (j // 128), j % 128]
            so_far = acc[jnp.maximum(prev, 0), pl.ds(0, size), :]
            acc[i, pl.ds(0, size), :] = r_bufs[q][i].astype(F32) + jnp.where(
                prev >= 0, so_far, 0.0
            )
            return 0

        lax.fori_loop(0, TILES, add_step, 0)
        p_cps[q].wait()

        def out_step(p, _):
            last = got_s[0, p]
            total = acc[jnp.maximum(last, 0), pl.ds(0, size), :]
            cols = pl.ds(pl.multiple_of((p % SIDE) * NB, NB), NB)
            p_bufs[q][p // SIDE, :, cols] = (
                p_bufs[q][p // SIDE, :, cols].astype(F32) + jnp.where(last >= 0, total, 0.0)
            ).astype(BF16)
            return 0

        lax.fori_loop(0, TILES, out_step, 0)
        o_cp = pltpu.make_async_copy(p_bufs[q], out.at[:, rows(q), :], o_sem.at[q])
        o_cp.start()
        o_cps.append(o_cp)

    for cp in f_cps + o_cps:
        cp.wait()
    for d in ORDER:
        pos_copy(d).wait_send()
        for q in range(NQ):
            x_copy(q, d).wait_send()

    @pl.when((r == 0) & (c == 0))
    def _():
        for row in range(2):
            for i in range(2):
                dt_copy(i, row).wait_send()

    @pl.when(r == 0)
    def _():
        b_copy.wait_send()

    for row in range(2):

        @pl.when((r == row) & (c == 0))
        def _():
            for q in range(NQ):
                c_copy(q, 1 - row).wait_send()


def body(front, inverses, routes, positions, parent):
    hbm = pl.BlockSpec(memory_space=pl.ANY)
    smem = pl.BlockSpec(memory_space=pltpu.SMEM)
    most = max(CHUNKS)
    dma = pltpu.SemaphoreType.DMA

    def per_chunk(shape):
        return [pltpu.VMEM(shape(n), BF16) for n in CHUNKS]

    scratch = (
        per_chunk(lambda n: (SIDE, n, 2 * NB))
        + per_chunk(lambda n: (SIDE, n, WIDTH))
        + per_chunk(lambda n: (SIDE, n, WIDTH))
        + per_chunk(lambda n: (SIDE, n, NB))
        + per_chunk(lambda n: (TILES, n, NB))
        + per_chunk(lambda n: (TILES, n, NB))
        + [
            pltpu.VMEM((2, NB, WIDTH), BF16),
            pltpu.VMEM((2, NB, NB), BF16),
            pltpu.VMEM((SIDE * most, 2 * NB), BF16),
            pltpu.VMEM((TILES, most, NB), BF16),
            pltpu.VMEM((TILES, most, NB), F32),
            pltpu.VMEM((GROUPS * 8, 128), jnp.int32),
            pltpu.VMEM((GROUPS * 8, 128), jnp.int32),
            pltpu.VMEM((8, 128), jnp.int32),
            pltpu.SMEM((8, 128), jnp.int32),
            pltpu.VMEM((24, 128), jnp.int32),
            pltpu.SMEM((24, 128), jnp.int32),
        ]
        + [dma((NQ,))] * 6
        + [dma((NQ, GROUPS))] * 2
        + [dma((GROUPS,))] * 2
        + [dma, dma, dma((2, 2)), dma((2,)), dma((2,))]
    )
    factor, added = pl.pallas_call(
        kernel,
        out_shape=(
            jax.ShapeDtypeStruct((SIDE, NB, NB), BF16),
            jax.ShapeDtypeStruct((SIDE, NB, WIDTH), BF16),
        ),
        in_specs=[hbm, pl.BlockSpec(memory_space=pltpu.VMEM), smem, smem, hbm],
        out_specs=(hbm, hbm),
        scratch_shapes=scratch,
        compiler_params=pltpu.CompilerParams(
            collective_id=0, has_side_effects=True, vmem_limit_bytes=60 * 2**20
        ),
        cost_estimate=pl.CostEstimate(
            flops=2 * WIDTH * WIDTH * 2 * NB, bytes_accessed=25 * 2**20, transcendentals=0
        ),
        name="eliminate_exchange_add",
    )(
        front.reshape(SIDE, NB, WIDTH),
        inverses[0],
        routes[0],
        positions[0],
        parent.reshape(SIDE, NB, WIDTH),
    )
    return factor.reshape(1, WIDTH, NB), added.reshape(1, WIDTH, WIDTH)


def solution(mesh):
    return jax.shard_map(
        body,
        mesh=mesh,
        in_specs=(
            P("front", "row", "col"),
            P("front", None, None, None),
            P("front", "row", "col"),
            P("front", "row", "col"),
            P("front", "row", "col"),
        ),
        out_specs=(P("front", "row", "col"), P("front", "row", "col")),
        check_vma=False,
    )
```

```python
import functools

import jax
import jax.numpy as jnp
from jax import lax
from jax.experimental import pallas as pl
from jax.experimental.pallas import tpu as pltpu
from jax.sharding import PartitionSpec as P

MESH = pl.DeviceIdType.MESH
NB = 256
SIDE = 8
TILES = SIDE * SIDE
GROUPS = 32
WIDTH = SIDE * NB
CHUNKS = (16, 32, 64, 48, 48, 32, 16)
RELAY = (4, 5, 6)
STARTS = tuple(sum(CHUNKS[:q]) for q in range(len(CHUNKS)))
NQ = len(CHUNKS)
F32 = jnp.float32
BF16 = jnp.bfloat16


def hops(d):
    return min(d[0], 4 - d[0]) + min(d[1], 4 - d[1]) + d[2]


OFFSETS = [(z, y, x) for z in range(4) for y in range(4) for x in range(2)]
STRAIGHT = sorted([d for d in OFFSETS[1:] if d[2] == 0], key=lambda d: -hops(d))
ACROSS = sorted([d for d in OFFSETS if d[2] == 1], key=lambda d: -hops(d))
ORDER = ACROSS + STRAIGHT
HELD = min(RELAY)


def dot(a, b):
    return jnp.dot(a, b, preferred_element_type=F32)


def chain(got, arrived, acc, size):
    def step(i, _):
        j = (i // 2) * 8 + i % 2
        prev = got[8 + 8 * (j // 128), j % 128]
        so_far = acc[jnp.maximum(prev, 0), pl.ds(0, size), :]
        acc[i, pl.ds(0, size), :] = arrived[i].astype(F32) + jnp.where(prev >= 0, so_far, 0.0)
        return 0

    lax.fori_loop(0, TILES, step, 0)


def place_all(got, acc, base, size):
    def step(p, _):
        last = got[0, p]
        total = acc[jnp.maximum(last, 0), pl.ds(0, size), :]
        cols = pl.ds(pl.multiple_of((p % SIDE) * NB, NB), NB)
        base[p // SIDE, :, cols] = (
            base[p // SIDE, :, cols].astype(F32) + jnp.where(last >= 0, total, 0.0)
        ).astype(BF16)
        return 0

    lax.fori_loop(0, TILES, step, 0)


def kernel(front, inv, routes, places, parent, fac_out, out, *refs):
    refs = list(refs)

    def take(n):
        got = refs[:n]
        del refs[:n]
        return got

    c_bufs, a_bufs, s_bufs, r_bufs = (take(NQ) for _ in range(4))
    by_bufs = dict(zip(RELAY, take(len(RELAY)), strict=True))
    (b_buf, dt, l_buf, tiles, acc, pos_send, pos_recv, tab_v, tab_s, got_v, got_s) = take(11)
    (c_ss, c_rs, a_sem, p_sem, x_ss, x_rs, pos_ss, pos_rs) = take(8)
    (b_ss, b_rs, dt_ss, dt_rs, t_sem, by_ss, by_rs) = take(7)

    me = lax.axis_index("front")
    r = lax.axis_index("row")
    c = lax.axis_index("col")
    z, y, x = me // 8, (me // 2) % 4, me % 2
    sign = jnp.where(r == 0, 1, 3)

    def peer(d):
        return ((z + sign * d[0]) % 4) * 8 + ((y + sign * d[1]) % 4) * 2 + (x + d[2]) % 2

    def rows(q):
        return pl.ds(STARTS[q], CHUNKS[q])

    a_cps = [
        pltpu.make_async_copy(front.at[:, rows(q), :], a_bufs[q], a_sem.at[q]) for q in range(NQ)
    ]
    p_cps = [
        pltpu.make_async_copy(parent.at[:, rows(q), :], out.at[:, rows(q), :], p_sem.at[q])
        for q in range(NQ)
    ]
    c_loc = [
        pltpu.make_async_copy(front.at[:, rows(q), pl.ds(0, 2 * NB)], c_bufs[q], c_rs.at[q])
        for q in range(NQ)
    ]
    b_loc = pltpu.make_async_copy(front.at[pl.ds(0, 2)], b_buf, b_rs)

    @pl.when(r == 0)
    def _():
        b_loc.start()

    @pl.when(c == 0)
    def _():
        c_loc[0].start()

    a_cps[0].start()

    bar = pltpu.get_barrier_semaphore()

    def greet(k, _):
        pl.semaphore_signal(
            bar, 1, device_id=((me + k) % GROUPS, r, c), device_id_type=MESH
        )
        return 0

    lax.fori_loop(1, GROUPS, greet, 0)
    pl.semaphore_signal(bar, 1, device_id=(me, 1 - r, c), device_id_type=MESH)
    pl.semaphore_signal(bar, 1, device_id=(me, r, 1 - c), device_id_type=MESH)
    pl.semaphore_signal(bar, 1, device_id=(me, 1 - r, 1 - c), device_id_type=MESH)
    other = me + 1 - 2 * x
    pl.semaphore_signal(bar, 1, device_id=(other, r, 1 - c), device_id_type=MESH)

    lane = lax.broadcasted_iota(jnp.int32, (TILES, 128), 1)
    sub = lax.broadcasted_iota(jnp.int32, (TILES, 128), 0)
    lane1 = lax.broadcasted_iota(jnp.int32, (1, 128), 1)

    def spread(t, carry):
        across, down, place = carry
        route = routes[t // SIDE, t % SIDE]
        across = jnp.where(lane1 == t, route, across)
        down = jnp.where(sub == t, route, down)
        place = jnp.where(lane1 == t, places[t // SIDE, t % SIDE], place)
        return across, down, place

    none1 = jnp.full((1, 128), -1, jnp.int32)
    across, down, place = lax.fori_loop(
        0, TILES, spread, (none1, jnp.full((TILES, 128), -1, jnp.int32), none1)
    )
    same = down == across
    before = jnp.sum(jnp.where(same & (sub < lane), 1, 0), axis=0, keepdims=True)
    slot8 = jnp.where((across >= 0) & (before < 2), across * 8 + before, -1)
    sub8 = lax.broadcasted_iota(jnp.int32, (GROUPS * 8, 128), 0)
    pos = jnp.max(jnp.where(slot8 == sub8, place, -1), axis=1, keepdims=True)
    pos_send[...] = jnp.broadcast_to(pos, (GROUPS * 8, 128))
    before = jnp.sum(jnp.where(same & (lane < sub), 1, 0), axis=1, keepdims=True)
    slot2 = jnp.where(down >= 0, down * 2 + before, -1)
    tab_v[...] = jnp.broadcast_to(
        jnp.max(jnp.where(slot2 == lane, sub, 0), axis=0, keepdims=True), (8, 128)
    )
    tab_cp = pltpu.make_async_copy(tab_v, tab_s, t_sem.at[0])
    tab_cp.start()
    pos_recv[pl.ds(0, 8), :] = pos_send[pl.ds(pl.multiple_of(me * 8, 8), 8), :]

    pl.semaphore_wait(bar, GROUPS + 3)

    def dt_copy(i, row):
        if i == 0:
            src = front.at[0, :, pl.ds(NB, NB)]
        else:
            src = front.at[1, :, pl.ds(0, NB)]
        return pltpu.make_async_remote_copy(
            src, dt.at[i], dt_ss.at[i, row], dt_rs.at[i], device_id=(me, row, 1), device_id_type=MESH
        )

    def c_copy(q, low):
        return pltpu.make_async_remote_copy(
            front.at[pl.ds(low, SIDE - low), rows(q), pl.ds(0, 2 * NB)],
            (by_bufs if q in RELAY else c_bufs)[q].at[pl.ds(low, SIDE - low)],
            c_ss.at[q],
            (by_rs if q in RELAY else c_rs).at[q],
            device_id=(other if q in RELAY else me, r, 1),
            device_id_type=MESH,
        )

    def by_copy(q, low):
        return pltpu.make_async_remote_copy(
            by_bufs[q].at[pl.ds(low, SIDE - low)],
            c_bufs[q].at[pl.ds(low, SIDE - low)],
            by_ss.at[q],
            c_rs.at[q],
            device_id=(other, r, 1),
            device_id_type=MESH,
        )

    def send_columns(q):
        for row in range(2):

            @pl.when((r == row) & (c == 0))
            def _():
                if q == 1:
                    c_copy(0, 1 - row).wait_send()
                if q > 2:
                    c_copy(q - 2, 1 - row).wait_send()
                c_copy(q, 1 - row).start()

    def forward(q):
        for row in range(2):

            @pl.when((r == row) & (c == 1))
            def _():
                c_copy(q, 1 - row).wait_recv()
                by_copy(q, 1 - row).start()

    b_copy = pltpu.make_async_remote_copy(
        front.at[pl.ds(0, 2)], b_buf, b_ss, b_rs, device_id=(me, 1, c), device_id_type=MESH
    )

    @pl.when((r == 0) & (c == 0))
    def _():
        for row in range(2):
            for i in range(2):
                dt_copy(i, row).start()

    @pl.when(r == 0)
    def _():
        b_copy.start()

    send_columns(0)

    for q in range(1, NQ):

        @pl.when(c == 0)
        def _():
            c_loc[q].start()

        a_cps[q].start()

    @pl.when((r == 0) & (c == 1))
    def _():
        for q in range(NQ):
            c_bufs[q][0] = jnp.zeros((CHUNKS[q], 2 * NB), BF16)

    def pos_copy(d):
        k = OFFSETS.index(d)
        g = peer(d)
        return pltpu.make_async_remote_copy(
            pos_send.at[pl.ds(pl.multiple_of(g * 8, 8), 8)],
            pos_recv.at[pl.ds(8 * k, 8)],
            pos_ss,
            pos_rs,
            device_id=(g, r, c),
            device_id_type=MESH,
        )

    @pl.when(r == 0)
    def _():
        b_loc.wait()

    @pl.when(r == 1)
    def _():
        b_copy.wait_recv()

    @pl.when(c == 0)
    def _():
        dt[0] = b_buf[0, :, pl.ds(NB, NB)]
        dt[1] = b_buf[1, :, pl.ds(0, NB)]

    @pl.when(c == 1)
    def _():
        for i in range(2):
            dt_copy(i, 0).wait_recv()

    panel_d = dot(dt[1], inv[0]).astype(BF16)

    def row_step(j, _):
        cols = pl.ds(pl.multiple_of(j * NB, NB), NB)
        b_buf[1, :, cols] = (
            b_buf[1, :, cols].astype(F32) - dot(panel_d, b_buf[0, :, cols])
        ).astype(BF16)
        return 0

    lax.fori_loop(0, SIDE, row_step, 0)
    send_columns(1)
    tab_cp.wait()

    def x_copy(q, d):
        k = OFFSETS.index(d)
        return pltpu.make_async_remote_copy(
            s_bufs[q].at[pl.ds(2 * k, 2)],
            r_bufs[q].at[pl.ds(2 * k, 2)],
            x_ss.at[q],
            x_rs.at[q],
            device_id=(peer(d), r, c),
            device_id_type=MESH,
        )

    for q in range(NQ):
        size = CHUNKS[q]

        @pl.when(c == 0)
        def _():
            c_loc[q].wait()

        for row in range(2):

            @pl.when((r == row) & (c == 1))
            def _():
                (by_copy if q in RELAY else c_copy)(q, 1 - row).wait_recv()

        first = c_bufs[q][:, :, pl.ds(0, NB)].reshape(SIDE * size, NB)
        second = c_bufs[q][:, :, pl.ds(NB, NB)].reshape(SIDE * size, NB)
        panel0 = dot(first, inv[0]).astype(BF16)
        second = (second.astype(F32) - dot(panel0, dt[0])).astype(BF16)
        panel1 = dot(second, inv[1])
        line = lax.broadcasted_iota(jnp.int32, panel1.shape, 0)
        panel1 = jnp.where((line < size) & (r == 0), 0.0, panel1).astype(BF16)
        l_buf[pl.ds(0, SIDE * size), pl.ds(0, NB)] = panel0
        l_buf[pl.ds(0, SIDE * size), pl.ds(NB, NB)] = panel1

        @pl.when(c == 0)
        def _():
            fac_out[:, rows(q), :] = panel0.reshape(SIDE, size, NB)

        @pl.when(c == 1)
        def _():
            fac_out[:, rows(q), :] = panel1.reshape(SIDE, size, NB)

        a_cps[q].wait()

        def tile_step(j, _):
            cols = pl.ds(pl.multiple_of(j * NB, NB), NB)
            both = b_buf[:, :, cols].reshape(2 * NB, NB)
            prod = dot(l_buf[pl.ds(0, SIDE * size), :], both)
            block = a_bufs[q][:, :, cols].astype(F32).reshape(SIDE * size, NB)
            block = (block - prod).astype(BF16).reshape(SIDE, size, NB)
            for i in range(SIDE):
                tiles[i * SIDE + j, pl.ds(0, size), :] = block[i]
            return 0

        lax.fori_loop(0, SIDE, tile_step, 0)

        for s in range(2):
            r_bufs[q][s] = tiles[tab_s[0, 2 * me + s], pl.ds(0, size), :]
        for d in STRAIGHT + ACROSS if q < HELD else ORDER:
            k = OFFSETS.index(d)
            g = peer(d)
            for s in range(2):
                s_bufs[q][2 * k + s] = tiles[tab_s[0, 2 * g + s], pl.ds(0, size), :]
            if q < HELD and d in ACROSS:

                @pl.when(c == 1)
                def _():
                    x_copy(q, d).start()

            else:
                x_copy(q, d).start()
        if q == 0:
            for d in ORDER:
                pos_copy(d).start()
            for cp in p_cps:
                cp.start()
        if q + 2 < NQ:
            send_columns(q + 2)
        if q == HELD - 1:
            for by in RELAY:
                forward(by)

            @pl.when(c == 0)
            def _():
                for early in range(HELD):
                    for d in ACROSS:
                        x_copy(early, d).start()

    def all_pos():
        some = pl.ds(8, 8 * (GROUPS - 1))
        return pltpu.make_async_remote_copy(
            pos_send.at[some],
            pos_recv.at[some],
            pos_ss,
            pos_rs,
            device_id=(other, r, c),
            device_id_type=MESH,
        )

    def all_x(q):
        some = pl.ds(2, 2 * (GROUPS - 1))
        return pltpu.make_async_remote_copy(
            s_bufs[q].at[some],
            r_bufs[q].at[some],
            x_ss.at[q],
            x_rs.at[q],
            device_id=(other, r, c),
            device_id_type=MESH,
        )

    all_pos().wait_recv()
    got = pos_recv[...]
    lane8 = lax.broadcasted_iota(jnp.int32, (GROUPS * 8, 128), 1)

    def slot_of(v):
        return jnp.where(v >= 0, (v >> 3) * 2 + (v & 1), -1)

    last = jnp.max(jnp.where(got == lane8, sub8, -1), axis=0, keepdims=True)
    got_v[pl.ds(0, 8), :] = jnp.broadcast_to(slot_of(last), (8, 128))
    eye = lax.broadcasted_iota(jnp.int32, (128, 128), 0) == lax.broadcasted_iota(
        jnp.int32, (128, 128), 1
    )
    for h in range(2):
        own = jnp.sum(
            jnp.where(eye, got[h * 128 : (h + 1) * 128], 0), axis=0, keepdims=True
        )
        prev = jnp.max(
            jnp.where((got == own) & (sub8 < lane8 + h * 128), sub8, -1), axis=0, keepdims=True
        )
        prev = jnp.where(own >= 0, prev, -1)
        got_v[pl.ds(8 + 8 * h, 8), :] = jnp.broadcast_to(slot_of(prev), (8, 128))
    got_cp = pltpu.make_async_copy(got_v, got_s, t_sem.at[1])
    got_cp.start()
    got_cp.wait()
    all_pos().wait_send()
    @pl.when((r == 0) & (c == 0))
    def _():
        for row in range(2):
            for i in range(2):
                dt_copy(i, row).wait_send()

    @pl.when(r == 0)
    def _():
        b_copy.wait_send()

    for row in range(2):

        @pl.when((r == row) & (c == 0))
        def _():
            for q in range(NQ - 2, NQ):
                c_copy(q, 1 - row).wait_send()

        @pl.when((r == row) & (c == 1))
        def _():
            for q in RELAY:
                by_copy(q, 1 - row).wait_send()

    for q in range(NQ):
        if q == NQ - 1:
            for sent in range(NQ - 1):
                all_x(sent).wait_send()
        all_x(q).wait_recv()
        chain(got_s, r_bufs[q], acc, CHUNKS[q])
        p_cps[q].wait()
        place_all(got_s, acc, out.at[:, rows(q), :], CHUNKS[q])
    all_x(NQ - 1).wait_send()


def body(front, inverses, routes, positions, parent):
    hbm = pl.BlockSpec(memory_space=pl.ANY)
    smem = pl.BlockSpec(memory_space=pltpu.SMEM)
    vmem = pl.BlockSpec(memory_space=pltpu.VMEM)
    most = max(CHUNKS)
    dma = pltpu.SemaphoreType.DMA

    def per_chunk(shape, chunks=CHUNKS):
        return [pltpu.VMEM(shape(n), BF16) for n in chunks]

    scratch = (
        per_chunk(lambda n: (SIDE, n, 2 * NB))
        + per_chunk(lambda n: (SIDE, n, WIDTH))
        + per_chunk(lambda n: (TILES, n, NB))
        + per_chunk(lambda n: (TILES, n, NB))
        + per_chunk(lambda n: (SIDE, n, 2 * NB), [CHUNKS[q] for q in RELAY])
        + [
            pltpu.VMEM((2, NB, WIDTH), BF16),
            pltpu.VMEM((2, NB, NB), BF16),
            pltpu.VMEM((SIDE * most, 2 * NB), BF16),
            pltpu.VMEM((TILES, most, NB), BF16),
            pltpu.VMEM((TILES, most, NB), F32),
            pltpu.VMEM((GROUPS * 8, 128), jnp.int32),
            pltpu.VMEM((GROUPS * 8, 128), jnp.int32),
            pltpu.VMEM((8, 128), jnp.int32),
            pltpu.SMEM((8, 128), jnp.int32),
            pltpu.VMEM((24, 128), jnp.int32),
            pltpu.SMEM((24, 128), jnp.int32),
        ]
        + [dma((NQ,))] * 6
        + [dma, dma]
        + [dma, dma, dma((2, 2)), dma((2,)), dma((2,)), dma((NQ,)), dma((NQ,))]
    )
    factor, added = pl.pallas_call(
        kernel,
        out_shape=(
            pltpu.VMEM((SIDE, NB, NB), BF16),
            pltpu.VMEM((SIDE, NB, WIDTH), BF16),
        ),
        in_specs=[hbm, vmem, smem, smem, hbm],
        out_specs=(vmem, vmem),
        scratch_shapes=scratch,
        compiler_params=pltpu.CompilerParams(
            collective_id=0, has_side_effects=True, vmem_limit_bytes=50 * 2**20
        ),
        cost_estimate=pl.CostEstimate(
            flops=2 * WIDTH * WIDTH * 2 * NB, bytes_accessed=25 * 2**20, transcendentals=0
        ),
        name="eliminate_exchange_add",
    )(
        front.reshape(SIDE, NB, WIDTH),
        inverses[0],
        routes[0],
        positions[0],
        parent.reshape(SIDE, NB, WIDTH),
    )
    return factor.reshape(1, WIDTH, NB), added.reshape(1, WIDTH, WIDTH)


def solution(mesh):
    return jax.shard_map(
        body,
        mesh=mesh,
        in_specs=(
            P("front", "row", "col"),
            P("front", None, None, None),
            P("front", "row", "col"),
            P("front", "row", "col"),
            P("front", "row", "col"),
        ),
        out_specs=(P("front", "row", "col"), P("front", "row", "col")),
        check_vma=False,
    )
```

```python
import functools

import jax
import jax.numpy as jnp
from jax import lax
from jax.experimental import pallas as pl
from jax.experimental.pallas import tpu as pltpu
from jax.sharding import PartitionSpec as P

MESH = pl.DeviceIdType.MESH
NB = 256
SIDE = 8
TILES = SIDE * SIDE
GROUPS = 32
WIDTH = SIDE * NB
CHUNKS = (16, 48, 48, 48, 64, 32)
RELAY = (4, 5)
STARTS = tuple(sum(CHUNKS[:q]) for q in range(len(CHUNKS)))
NQ = len(CHUNKS)
LAST = CHUNKS[-1]
F32 = jnp.float32
BF16 = jnp.bfloat16


def hops(d):
    return min(d[0], 4 - d[0]) + min(d[1], 4 - d[1]) + d[2]


OFFSETS = [(z, y, x) for z in range(4) for y in range(4) for x in range(2)]
STRAIGHT = sorted([d for d in OFFSETS[1:] if d[2] == 0], key=lambda d: -hops(d))
ACROSS = sorted([d for d in OFFSETS if d[2] == 1], key=lambda d: -hops(d))
ORDER = ACROSS + STRAIGHT
HELD = min(RELAY) - 1


def dot(a, b):
    return jnp.dot(a, b, preferred_element_type=F32)


def chain(got, arrived, acc, size):
    def step(i, _):
        j = (i // 2) * 8 + i % 2
        prev = got[8 + 8 * (j // 128), j % 128]
        so_far = acc[jnp.maximum(prev, 0), pl.ds(0, size), :]
        acc[i, pl.ds(0, size), :] = arrived[i].astype(F32) + jnp.where(prev >= 0, so_far, 0.0)
        return 0

    lax.fori_loop(0, TILES, step, 0)


def place_all(got, acc, base, to, size):
    def step(p, _):
        last = got[0, p]
        total = acc[jnp.maximum(last, 0), pl.ds(0, size), :]
        cols = pl.ds(pl.multiple_of((p % SIDE) * NB, NB), NB)
        to[p // SIDE, :, cols] = (
            base[p // SIDE, :, cols].astype(F32) + jnp.where(last >= 0, total, 0.0)
        ).astype(BF16)
        return 0

    lax.fori_loop(0, TILES, step, 0)


def kernel(front, inv, routes, places, parent, fac_out, out, last_out, got_v, *refs):
    refs = list(refs)

    def take(n):
        got = refs[:n]
        del refs[:n]
        return got

    c_bufs, a_bufs, s_bufs = (take(NQ) for _ in range(3))
    r_bufs = take(NQ - 1) + [last_out]
    by_bufs = dict(zip(RELAY, take(len(RELAY)), strict=True))
    (b_buf, dt, l_buf, tiles, acc, pos_send, pos_recv, tab_v, tab_s, got_s) = take(10)
    (c_ss, c_rs, a_sem, p_sem, x_ss, x_rs, pos_ss, pos_rs) = take(8)
    (b_ss, b_rs, dt_ss, dt_rs, t_sem, by_ss, by_rs) = take(7)

    me = lax.axis_index("front")
    r = lax.axis_index("row")
    c = lax.axis_index("col")
    z, y, x = me // 8, (me // 2) % 4, me % 2
    sign = jnp.where(r == 0, 1, 3)

    def peer(d):
        return ((z + sign * d[0]) % 4) * 8 + ((y + sign * d[1]) % 4) * 2 + (x + d[2]) % 2

    def rows(q):
        return pl.ds(STARTS[q], CHUNKS[q])

    a_cps = [
        pltpu.make_async_copy(front.at[:, rows(q), :], a_bufs[q], a_sem.at[q]) for q in range(NQ)
    ]
    p_cps = [
        pltpu.make_async_copy(parent.at[:, rows(q), :], out.at[:, rows(q), :], p_sem.at[q])
        for q in range(NQ)
    ]
    c_loc = [
        pltpu.make_async_copy(front.at[:, rows(q), pl.ds(0, 2 * NB)], c_bufs[q], c_rs.at[q])
        for q in range(NQ)
    ]
    b_loc = pltpu.make_async_copy(front.at[pl.ds(0, 2)], b_buf, b_rs)

    @pl.when(r == 0)
    def _():
        b_loc.start()

    @pl.when(c == 0)
    def _():
        c_loc[0].start()

    a_cps[0].start()

    bar = pltpu.get_barrier_semaphore()

    def greet(k, _):
        pl.semaphore_signal(
            bar, 1, device_id=((me + k) % GROUPS, r, c), device_id_type=MESH
        )
        return 0

    lax.fori_loop(1, GROUPS, greet, 0)
    pl.semaphore_signal(bar, 1, device_id=(me, 1 - r, c), device_id_type=MESH)
    pl.semaphore_signal(bar, 1, device_id=(me, r, 1 - c), device_id_type=MESH)
    pl.semaphore_signal(bar, 1, device_id=(me, 1 - r, 1 - c), device_id_type=MESH)
    other = me + 1 - 2 * x
    pl.semaphore_signal(bar, 1, device_id=(other, r, 1 - c), device_id_type=MESH)

    pl.semaphore_wait(bar, GROUPS + 3)

    def dt_copy(i):
        if i == 0:
            src = front.at[0, :, pl.ds(NB, NB)]
        else:
            src = front.at[1, :, pl.ds(0, NB)]
        return pltpu.make_async_remote_copy(
            src, dt.at[i], dt_ss.at[i], dt_rs.at[i], device_id=(me, 0, 1), device_id_type=MESH
        )

    def dt_pass(i):
        return pltpu.make_async_remote_copy(
            dt.at[i], dt.at[i], dt_ss.at[i], dt_rs.at[i], device_id=(me, 1, 1), device_id_type=MESH
        )

    def c_copy(q, low):
        return pltpu.make_async_remote_copy(
            front.at[pl.ds(low, SIDE - low), rows(q), pl.ds(0, 2 * NB)],
            (by_bufs if q in RELAY else c_bufs)[q].at[pl.ds(low, SIDE - low)],
            c_ss.at[q],
            (by_rs if q in RELAY else c_rs).at[q],
            device_id=(other if q in RELAY else me, r, 1),
            device_id_type=MESH,
        )

    def by_copy(q, low):
        return pltpu.make_async_remote_copy(
            by_bufs[q].at[pl.ds(low, SIDE - low)],
            c_bufs[q].at[pl.ds(low, SIDE - low)],
            by_ss.at[q],
            c_rs.at[q],
            device_id=(other, r, 1),
            device_id_type=MESH,
        )

    left = []

    def send_columns(send, after):
        for row in range(2):

            @pl.when((r == row) & (c == 0))
            def _():
                for q in after:
                    c_copy(q, 1 - row).wait_send()
                for q in send:
                    c_copy(q, 1 - row).start()

        left.extend(after)

    def forward(q):
        for row in range(2):

            @pl.when((r == row) & (c == 1))
            def _():
                c_copy(q, 1 - row).wait_recv()
                by_copy(q, 1 - row).start()

    b_copy = pltpu.make_async_remote_copy(
        front.at[pl.ds(0, 2)], b_buf, b_ss, b_rs, device_id=(me, 1, c), device_id_type=MESH
    )

    @pl.when((r == 0) & (c == 0))
    def _():
        for i in range(2):
            dt_copy(i).start()

    @pl.when(r == 0)
    def _():
        b_copy.start()

    send_columns([0], [])

    lane = lax.broadcasted_iota(jnp.int32, (TILES, 128), 1)
    sub = lax.broadcasted_iota(jnp.int32, (TILES, 128), 0)
    lane1 = lax.broadcasted_iota(jnp.int32, (1, 128), 1)

    def spread(t, carry):
        across, down, place = carry
        route = routes[t // SIDE, t % SIDE]
        across = jnp.where(lane1 == t, route, across)
        down = jnp.where(sub == t, route, down)
        place = jnp.where(lane1 == t, places[t // SIDE, t % SIDE], place)
        return across, down, place

    none1 = jnp.full((1, 128), -1, jnp.int32)
    across, down, place = lax.fori_loop(
        0, TILES, spread, (none1, jnp.full((TILES, 128), -1, jnp.int32), none1)
    )
    same = down == across
    before = jnp.sum(jnp.where(same & (sub < lane), 1, 0), axis=0, keepdims=True)
    slot8 = jnp.where((across >= 0) & (before < 2), across * 8 + before, -1)
    sub8 = lax.broadcasted_iota(jnp.int32, (GROUPS * 8, 128), 0)
    pos = jnp.max(jnp.where(slot8 == sub8, place, -1), axis=1, keepdims=True)
    pos_send[...] = jnp.broadcast_to(pos, (GROUPS * 8, 128))
    before = jnp.sum(jnp.where(same & (lane < sub), 1, 0), axis=1, keepdims=True)
    slot2 = jnp.where(down >= 0, down * 2 + before, -1)
    tab_v[...] = jnp.broadcast_to(
        jnp.max(jnp.where(slot2 == lane, sub, 0), axis=0, keepdims=True), (8, 128)
    )
    tab_cp = pltpu.make_async_copy(tab_v, tab_s, t_sem.at[0])
    tab_cp.start()
    pos_recv[pl.ds(0, 8), :] = pos_send[pl.ds(pl.multiple_of(me * 8, 8), 8), :]

    send_columns([1], [0])

    for q in range(1, NQ):

        @pl.when(c == 0)
        def _():
            c_loc[q].start()

        a_cps[q].start()

    @pl.when((r == 0) & (c == 1))
    def _():
        for q in range(NQ):
            c_bufs[q][0] = jnp.zeros((CHUNKS[q], 2 * NB), BF16)

    def pos_copy(d):
        k = OFFSETS.index(d)
        g = peer(d)
        return pltpu.make_async_remote_copy(
            pos_send.at[pl.ds(pl.multiple_of(g * 8, 8), 8)],
            pos_recv.at[pl.ds(8 * k, 8)],
            pos_ss,
            pos_rs,
            device_id=(g, r, c),
            device_id_type=MESH,
        )

    @pl.when((r == 0) & (c == 1))
    def _():
        for i in range(2):
            dt_copy(i).wait_recv()
            dt_pass(i).start()

    @pl.when(r == 0)
    def _():
        b_loc.wait()

    @pl.when(r == 1)
    def _():
        b_copy.wait_recv()

    @pl.when(c == 0)
    def _():
        dt[0] = b_buf[0, :, pl.ds(NB, NB)]
        dt[1] = b_buf[1, :, pl.ds(0, NB)]

    @pl.when((r == 1) & (c == 1))
    def _():
        for i in range(2):
            dt_pass(i).wait_recv()

    panel_d = dot(dt[1], inv[0]).astype(BF16)

    def row_step(j, _):
        cols = pl.ds(pl.multiple_of(j * NB, NB), NB)
        b_buf[1, :, cols] = (
            b_buf[1, :, cols].astype(F32) - dot(panel_d, b_buf[0, :, cols])
        ).astype(BF16)
        return 0

    lax.fori_loop(0, SIDE, row_step, 0)
    send_columns([2], [1])
    tab_cp.wait()

    def x_copy(q, d):
        k = OFFSETS.index(d)
        return pltpu.make_async_remote_copy(
            s_bufs[q].at[pl.ds(2 * k, 2)],
            r_bufs[q].at[pl.ds(2 * k, 2)],
            x_ss.at[q],
            x_rs.at[q],
            device_id=(peer(d), r, c),
            device_id_type=MESH,
        )

    for q in range(NQ):
        size = CHUNKS[q]

        @pl.when(c == 0)
        def _():
            c_loc[q].wait()

        for row in range(2):

            @pl.when((r == row) & (c == 1))
            def _():
                (by_copy if q in RELAY else c_copy)(q, 1 - row).wait_recv()

        first = c_bufs[q][:, :, pl.ds(0, NB)].reshape(SIDE * size, NB)
        second = c_bufs[q][:, :, pl.ds(NB, NB)].reshape(SIDE * size, NB)
        panel0 = dot(first, inv[0]).astype(BF16)
        second = (second.astype(F32) - dot(panel0, dt[0])).astype(BF16)
        panel1 = dot(second, inv[1])
        line = lax.broadcasted_iota(jnp.int32, panel1.shape, 0)
        panel1 = jnp.where((line < size) & (r == 0), 0.0, panel1).astype(BF16)
        l_buf[pl.ds(0, SIDE * size), pl.ds(0, NB)] = panel0
        l_buf[pl.ds(0, SIDE * size), pl.ds(NB, NB)] = panel1

        @pl.when(c == 0)
        def _():
            fac_out[:, rows(q), :] = panel0.reshape(SIDE, size, NB)

        @pl.when(c == 1)
        def _():
            fac_out[:, rows(q), :] = panel1.reshape(SIDE, size, NB)

        a_cps[q].wait()

        def tile_step(j, _):
            cols = pl.ds(pl.multiple_of(j * NB, NB), NB)
            both = b_buf[:, :, cols].reshape(2 * NB, NB)
            prod = dot(l_buf[pl.ds(0, SIDE * size), :], both)
            block = a_bufs[q][:, :, cols].astype(F32).reshape(SIDE * size, NB)
            block = (block - prod).astype(BF16).reshape(SIDE, size, NB)
            for i in range(SIDE):
                tiles[i * SIDE + j, pl.ds(0, size), :] = block[i]
            return 0

        lax.fori_loop(0, SIDE, tile_step, 0)

        for s in range(2):
            r_bufs[q][s] = tiles[tab_s[0, 2 * me + s], pl.ds(0, size), :]
        for d in ORDER:
            k = OFFSETS.index(d)
            g = peer(d)
            for s in range(2):
                s_bufs[q][2 * k + s] = tiles[tab_s[0, 2 * g + s], pl.ds(0, size), :]
            if q < HELD and d in ACROSS:

                @pl.when(c == 1)
                def _():
                    x_copy(q, d).start()

            else:
                x_copy(q, d).start()
        if q == 0:
            for d in ORDER:
                pos_copy(d).start()
            for cp in p_cps:
                cp.start()
        if q == 1:
            send_columns([3], [])
        if q == HELD - 1:
            send_columns([HELD + 1], range(2, HELD))
            send_columns([HELD + 2], [HELD])
        elif q >= HELD and q + 3 < NQ:
            send_columns([q + 3], [q + 1])
        if q == min(RELAY) - 1:
            for by in RELAY:
                forward(by)
        if q == HELD - 1:
            @pl.when(c == 0)
            def _():
                for early in range(HELD):
                    for d in ACROSS:
                        x_copy(early, d).start()

    def all_pos():
        some = pl.ds(8, 8 * (GROUPS - 1))
        return pltpu.make_async_remote_copy(
            pos_send.at[some],
            pos_recv.at[some],
            pos_ss,
            pos_rs,
            device_id=(other, r, c),
            device_id_type=MESH,
        )

    def all_x(q):
        some = pl.ds(2, 2 * (GROUPS - 1))
        return pltpu.make_async_remote_copy(
            s_bufs[q].at[some],
            r_bufs[q].at[some],
            x_ss.at[q],
            x_rs.at[q],
            device_id=(other, r, c),
            device_id_type=MESH,
        )

    all_pos().wait_recv()
    got = pos_recv[...]
    lane8 = lax.broadcasted_iota(jnp.int32, (GROUPS * 8, 128), 1)

    def slot_of(v):
        return jnp.where(v >= 0, (v >> 3) * 2 + (v & 1), -1)

    last = jnp.max(jnp.where(got == lane8, sub8, -1), axis=0, keepdims=True)
    got_v[pl.ds(0, 8), :] = jnp.broadcast_to(slot_of(last), (8, 128))
    eye = lax.broadcasted_iota(jnp.int32, (128, 128), 0) == lax.broadcasted_iota(
        jnp.int32, (128, 128), 1
    )
    for h in range(2):
        own = jnp.sum(
            jnp.where(eye, got[h * 128 : (h + 1) * 128], 0), axis=0, keepdims=True
        )
        prev = jnp.max(
            jnp.where((got == own) & (sub8 < lane8 + h * 128), sub8, -1), axis=0, keepdims=True
        )
        prev = jnp.where(own >= 0, prev, -1)
        got_v[pl.ds(8 + 8 * h, 8), :] = jnp.broadcast_to(slot_of(prev), (8, 128))
    got_cp = pltpu.make_async_copy(got_v, got_s, t_sem.at[1])
    got_cp.start()
    got_cp.wait()
    all_pos().wait_send()
    @pl.when((r == 0) & (c == 0))
    def _():
        for i in range(2):
            dt_copy(i).wait_send()

    @pl.when((r == 0) & (c == 1))
    def _():
        for i in range(2):
            dt_pass(i).wait_send()

    @pl.when(r == 0)
    def _():
        b_copy.wait_send()

    for row in range(2):

        @pl.when((r == row) & (c == 0))
        def _():
            for q in range(NQ):
                if q not in left:
                    c_copy(q, 1 - row).wait_send()

        @pl.when((r == row) & (c == 1))
        def _():
            for q in RELAY:
                by_copy(q, 1 - row).wait_send()

    for q in range(NQ):
        if q == NQ - 1:
            for sent in range(NQ - 1):
                all_x(sent).wait_send()
            p_cps[q].wait()
        all_x(q).wait_recv()
        if q < NQ - 1:
            chain(got_s, r_bufs[q], acc, CHUNKS[q])
            p_cps[q].wait()
            place_all(got_s, acc, out.at[:, rows(q), :], out.at[:, rows(q), :], CHUNKS[q])
    all_x(NQ - 1).wait_send()


def finish(factor, part, arrived, got, fac_out, out, got_s, acc, rest, sem):
    done = STARTS[-1]
    got_cp = pltpu.make_async_copy(got, got_s, sem.at[0])
    got_cp.start()
    moves = [pltpu.make_async_copy(factor, fac_out, sem.at[1])]
    for i in range(SIDE):
        ready = pl.ds(0, done)
        moves.append(
            pltpu.make_async_copy(part.at[i, ready, :], out.at[i, ready, :], sem.at[3 + i])
        )
    for cp in moves:
        cp.start()
    got_cp.wait()
    chain(got_s, arrived, acc, LAST)
    place_all(got_s, acc, part.at[:, pl.ds(done, LAST), :], rest, LAST)
    last_cp = pltpu.make_async_copy(rest, out.at[:, pl.ds(done, LAST), :], sem.at[2])
    last_cp.start()
    for cp in moves + [last_cp]:
        cp.wait()


def body(front, inverses, routes, positions, parent):
    hbm = pl.BlockSpec(memory_space=pl.ANY)
    smem = pl.BlockSpec(memory_space=pltpu.SMEM)
    vmem = pl.BlockSpec(memory_space=pltpu.VMEM)
    most = max(CHUNKS)
    dma = pltpu.SemaphoreType.DMA

    def per_chunk(shape, chunks=CHUNKS):
        return [pltpu.VMEM(shape(n), BF16) for n in chunks]

    scratch = (
        per_chunk(lambda n: (SIDE, n, 2 * NB))
        + per_chunk(lambda n: (SIDE, n, WIDTH))
        + per_chunk(lambda n: (TILES, n, NB))
        + per_chunk(lambda n: (TILES, n, NB), CHUNKS[:-1])
        + per_chunk(lambda n: (SIDE, n, 2 * NB), [CHUNKS[q] for q in RELAY])
        + [
            pltpu.VMEM((2, NB, WIDTH), BF16),
            pltpu.VMEM((2, NB, NB), BF16),
            pltpu.VMEM((SIDE * most, 2 * NB), BF16),
            pltpu.VMEM((TILES, most, NB), BF16),
            pltpu.VMEM((TILES, most, NB), F32),
            pltpu.VMEM((GROUPS * 8, 128), jnp.int32),
            pltpu.VMEM((GROUPS * 8, 128), jnp.int32),
            pltpu.VMEM((8, 128), jnp.int32),
            pltpu.SMEM((8, 128), jnp.int32),
            pltpu.SMEM((24, 128), jnp.int32),
        ]
        + [dma((NQ,))] * 6
        + [dma, dma]
        + [dma, dma, dma((2,)), dma((2,)), dma((2,)), dma((NQ,)), dma((NQ,))]
    )
    factor, part, arrived, got = pl.pallas_call(
        kernel,
        out_shape=(
            pltpu.VMEM((SIDE, NB, NB), BF16),
            pltpu.VMEM((SIDE, NB, WIDTH), BF16),
            pltpu.VMEM((TILES, LAST, NB), BF16),
            pltpu.VMEM((24, 128), jnp.int32),
        ),
        in_specs=[hbm, vmem, smem, smem, hbm],
        out_specs=(vmem,) * 4,
        scratch_shapes=scratch,
        compiler_params=pltpu.CompilerParams(
            collective_id=0, has_side_effects=True, vmem_limit_bytes=50 * 2**20
        ),
        cost_estimate=pl.CostEstimate(
            flops=2 * WIDTH * WIDTH * 2 * NB, bytes_accessed=25 * 2**20, transcendentals=0
        ),
        name="eliminate_exchange_add",
    )(
        front.reshape(SIDE, NB, WIDTH),
        inverses[0],
        routes[0],
        positions[0],
        parent.reshape(SIDE, NB, WIDTH),
    )
    factor, added = pl.pallas_call(
        finish,
        out_shape=(
            jax.ShapeDtypeStruct((SIDE, NB, NB), BF16),
            jax.ShapeDtypeStruct((SIDE, NB, WIDTH), BF16),
        ),
        in_specs=[vmem] * 4,
        out_specs=(hbm, hbm),
        scratch_shapes=[
            pltpu.SMEM((24, 128), jnp.int32),
            pltpu.VMEM((TILES, LAST, NB), F32),
            pltpu.VMEM((SIDE, LAST, WIDTH), BF16),
            dma((3 + SIDE,)),
        ],
        compiler_params=pltpu.CompilerParams(vmem_limit_bytes=30 * 2**20),
        cost_estimate=pl.CostEstimate(
            flops=2 * TILES * LAST * NB, bytes_accessed=10 * 2**20, transcendentals=0
        ),
        name="finish",
    )(factor, part, arrived, got)
    return factor.reshape(1, WIDTH, NB), added.reshape(1, WIDTH, WIDTH)


def solution(mesh):
    return jax.shard_map(
        body,
        mesh=mesh,
        in_specs=(
            P("front", "row", "col"),
            P("front", None, None, None),
            P("front", "row", "col"),
            P("front", "row", "col"),
            P("front", "row", "col"),
        ),
        out_specs=(P("front", "row", "col"), P("front", "row", "col")),
        check_vma=False,
    )
```

```python
import functools

import jax
import jax.numpy as jnp
from jax import lax
from jax.experimental import pallas as pl
from jax.experimental.pallas import tpu as pltpu
from jax.sharding import PartitionSpec as P

MESH = pl.DeviceIdType.MESH
NB = 256
SIDE = 8
TILES = SIDE * SIDE
GROUPS = 32
WIDTH = SIDE * NB
CHUNKS = (16, 48, 48, 48, 64, 32)
RELAY = (4, 5)
STARTS = tuple(sum(CHUNKS[:q]) for q in range(len(CHUNKS)))
NQ = len(CHUNKS)
LAST = CHUNKS[-1]
F32 = jnp.float32
BF16 = jnp.bfloat16


def hops(d):
    return min(d[0], 4 - d[0]) + min(d[1], 4 - d[1]) + d[2]


OFFSETS = [(z, y, x) for z in range(4) for y in range(4) for x in range(2)]
STRAIGHT = sorted([d for d in OFFSETS[1:] if d[2] == 0], key=lambda d: -hops(d))
ACROSS = sorted([d for d in OFFSETS if d[2] == 1], key=lambda d: -hops(d))
ORDER = ACROSS + STRAIGHT
HELD = min(RELAY) - 1


def dot(a, b):
    return jnp.dot(a, b, preferred_element_type=F32)


def chain(got, arrived, acc, size):
    def step(i, _):
        j = (i // 2) * 8 + i % 2
        prev = got[8 + 8 * (j // 128), j % 128]
        so_far = acc[jnp.maximum(prev, 0), pl.ds(0, size), :]
        acc[i, pl.ds(0, size), :] = arrived[i].astype(F32) + jnp.where(prev >= 0, so_far, 0.0)
        return 0

    lax.fori_loop(0, TILES, step, 0, unroll=4)


def place_all(got, acc, base, to, size):
    def step(p, _):
        last = got[0, p]
        total = acc[jnp.maximum(last, 0), pl.ds(0, size), :]
        cols = pl.ds(pl.multiple_of((p % SIDE) * NB, NB), NB)
        to[p // SIDE, :, cols] = (
            base[p // SIDE, :, cols].astype(F32) + jnp.where(last >= 0, total, 0.0)
        ).astype(BF16)
        return 0

    lax.fori_loop(0, TILES, step, 0, unroll=4)


def kernel(front, inv, routes, places, parent, fac_out, out, last_out, got_v, *refs):
    refs = list(refs)

    def take(n):
        got = refs[:n]
        del refs[:n]
        return got

    c_bufs, a_bufs, s_bufs = (take(NQ) for _ in range(3))
    r_bufs = take(NQ - 1) + [last_out]
    by_bufs = dict(zip(RELAY, take(len(RELAY)), strict=True))
    (b_buf, dt, l_buf, tiles, acc, pos_send, pos_recv, tab_v, tab_s, got_s) = take(10)
    (c_ss, c_rs, a_sem, p_sem, x_ss, x_rs, pos_ss, pos_rs) = take(8)
    (b_ss, b_rs, dt_ss, dt_rs, t_sem, by_ss, by_rs) = take(7)

    me = lax.axis_index("front")
    r = lax.axis_index("row")
    c = lax.axis_index("col")
    z, y, x = me // 8, (me // 2) % 4, me % 2
    sign = jnp.where(r == 0, 1, 3)

    def peer(d):
        return ((z + sign * d[0]) % 4) * 8 + ((y + sign * d[1]) % 4) * 2 + (x + d[2]) % 2

    def rows(q):
        return pl.ds(STARTS[q], CHUNKS[q])

    a_cps = [
        pltpu.make_async_copy(front.at[:, rows(q), :], a_bufs[q], a_sem.at[q]) for q in range(NQ)
    ]
    p_cps = [
        pltpu.make_async_copy(parent.at[:, rows(q), :], out.at[:, rows(q), :], p_sem.at[q])
        for q in range(NQ)
    ]
    c_loc = [
        pltpu.make_async_copy(front.at[:, rows(q), pl.ds(0, 2 * NB)], c_bufs[q], c_rs.at[q])
        for q in range(NQ)
    ]
    b_loc = pltpu.make_async_copy(front.at[pl.ds(0, 2)], b_buf, b_rs)

    @pl.when(r == 0)
    def _():
        b_loc.start()

    @pl.when(c == 0)
    def _():
        c_loc[0].start()

    a_cps[0].start()

    bar = pltpu.get_barrier_semaphore()

    def greet(k, _):
        pl.semaphore_signal(
            bar, 1, device_id=((me + k) % GROUPS, r, c), device_id_type=MESH
        )
        return 0

    lax.fori_loop(1, GROUPS, greet, 0)
    pl.semaphore_signal(bar, 1, device_id=(me, 1 - r, c), device_id_type=MESH)
    pl.semaphore_signal(bar, 1, device_id=(me, r, 1 - c), device_id_type=MESH)
    pl.semaphore_signal(bar, 1, device_id=(me, 1 - r, 1 - c), device_id_type=MESH)
    other = me + 1 - 2 * x
    pl.semaphore_signal(bar, 1, device_id=(other, r, 1 - c), device_id_type=MESH)

    pl.semaphore_wait(bar, GROUPS + 3)

    def dt_copy(i):
        if i == 0:
            src = front.at[0, :, pl.ds(NB, NB)]
        else:
            src = front.at[1, :, pl.ds(0, NB)]
        return pltpu.make_async_remote_copy(
            src, dt.at[i], dt_ss.at[i], dt_rs.at[i], device_id=(me, 0, 1), device_id_type=MESH
        )

    def dt_pass(i):
        return pltpu.make_async_remote_copy(
            dt.at[i], dt.at[i], dt_ss.at[i], dt_rs.at[i], device_id=(me, 1, 1), device_id_type=MESH
        )

    def c_copy(q, low):
        return pltpu.make_async_remote_copy(
            front.at[pl.ds(low, SIDE - low), rows(q), pl.ds(0, 2 * NB)],
            (by_bufs if q in RELAY else c_bufs)[q].at[pl.ds(low, SIDE - low)],
            c_ss.at[q],
            (by_rs if q in RELAY else c_rs).at[q],
            device_id=(other if q in RELAY else me, r, 1),
            device_id_type=MESH,
        )

    def by_copy(q, low):
        return pltpu.make_async_remote_copy(
            by_bufs[q].at[pl.ds(low, SIDE - low)],
            c_bufs[q].at[pl.ds(low, SIDE - low)],
            by_ss.at[q],
            c_rs.at[q],
            device_id=(other, r, 1),
            device_id_type=MESH,
        )

    left = []

    def send_columns(send, after):
        for row in range(2):

            @pl.when((r == row) & (c == 0))
            def _():
                for q in after:
                    c_copy(q, 1 - row).wait_send()
                for q in send:
                    c_copy(q, 1 - row).start()

        left.extend(after)

    def forward(q):
        for row in range(2):

            @pl.when((r == row) & (c == 1))
            def _():
                c_copy(q, 1 - row).wait_recv()
                by_copy(q, 1 - row).start()

    b_copy = pltpu.make_async_remote_copy(
        front.at[pl.ds(0, 2)], b_buf, b_ss, b_rs, device_id=(me, 1, c), device_id_type=MESH
    )

    @pl.when((r == 0) & (c == 0))
    def _():
        for i in range(2):
            dt_copy(i).start()

    @pl.when(r == 0)
    def _():
        b_copy.start()

    send_columns([0], [])

    lane = lax.broadcasted_iota(jnp.int32, (TILES, 128), 1)
    sub = lax.broadcasted_iota(jnp.int32, (TILES, 128), 0)
    lane1 = lax.broadcasted_iota(jnp.int32, (1, 128), 1)

    def spread(t, carry):
        across, down, place = carry
        route = routes[t // SIDE, t % SIDE]
        across = jnp.where(lane1 == t, route, across)
        down = jnp.where(sub == t, route, down)
        place = jnp.where(lane1 == t, places[t // SIDE, t % SIDE], place)
        return across, down, place

    none1 = jnp.full((1, 128), -1, jnp.int32)
    across, down, place = lax.fori_loop(
        0, TILES, spread, (none1, jnp.full((TILES, 128), -1, jnp.int32), none1)
    )
    same = down == across
    before = jnp.sum(jnp.where(same & (sub < lane), 1, 0), axis=0, keepdims=True)
    slot8 = jnp.where((across >= 0) & (before < 2), across * 8 + before, -1)
    sub8 = lax.broadcasted_iota(jnp.int32, (GROUPS * 8, 128), 0)
    pos = jnp.max(jnp.where(slot8 == sub8, place, -1), axis=1, keepdims=True)
    pos_send[...] = jnp.broadcast_to(pos, (GROUPS * 8, 128))
    before = jnp.sum(jnp.where(same & (lane < sub), 1, 0), axis=1, keepdims=True)
    slot2 = jnp.where(down >= 0, down * 2 + before, -1)
    tab_v[...] = jnp.broadcast_to(
        jnp.max(jnp.where(slot2 == lane, sub, 0), axis=0, keepdims=True), (8, 128)
    )
    tab_cp = pltpu.make_async_copy(tab_v, tab_s, t_sem.at[0])
    tab_cp.start()
    pos_recv[pl.ds(0, 8), :] = pos_send[pl.ds(pl.multiple_of(me * 8, 8), 8), :]

    send_columns([1], [0])

    for q in range(1, NQ):

        @pl.when(c == 0)
        def _():
            c_loc[q].start()

        a_cps[q].start()

    @pl.when((r == 0) & (c == 1))
    def _():
        for q in range(NQ):
            c_bufs[q][0] = jnp.zeros((CHUNKS[q], 2 * NB), BF16)

    def pos_copy(d):
        k = OFFSETS.index(d)
        g = peer(d)
        return pltpu.make_async_remote_copy(
            pos_send.at[pl.ds(pl.multiple_of(g * 8, 8), 8)],
            pos_recv.at[pl.ds(8 * k, 8)],
            pos_ss,
            pos_rs,
            device_id=(g, r, c),
            device_id_type=MESH,
        )

    @pl.when((r == 0) & (c == 1))
    def _():
        for i in range(2):
            dt_copy(i).wait_recv()
            dt_pass(i).start()

    @pl.when(r == 0)
    def _():
        b_loc.wait()

    @pl.when(r == 1)
    def _():
        b_copy.wait_recv()

    @pl.when(c == 0)
    def _():
        dt[0] = b_buf[0, :, pl.ds(NB, NB)]
        dt[1] = b_buf[1, :, pl.ds(0, NB)]

    @pl.when((r == 1) & (c == 1))
    def _():
        for i in range(2):
            dt_pass(i).wait_recv()

    panel_d = dot(dt[1], inv[0]).astype(BF16)

    def row_step(j, _):
        cols = pl.ds(pl.multiple_of(j * NB, NB), NB)
        b_buf[1, :, cols] = (
            b_buf[1, :, cols].astype(F32) - dot(panel_d, b_buf[0, :, cols])
        ).astype(BF16)
        return 0

    lax.fori_loop(0, SIDE, row_step, 0)
    send_columns([2], [1])
    tab_cp.wait()

    def x_copy(q, d):
        k = OFFSETS.index(d)
        return pltpu.make_async_remote_copy(
            s_bufs[q].at[pl.ds(2 * k, 2)],
            r_bufs[q].at[pl.ds(2 * k, 2)],
            x_ss.at[q],
            x_rs.at[q],
            device_id=(peer(d), r, c),
            device_id_type=MESH,
        )

    for q in range(NQ):
        size = CHUNKS[q]

        @pl.when(c == 0)
        def _():
            c_loc[q].wait()

        for row in range(2):

            @pl.when((r == row) & (c == 1))
            def _():
                (by_copy if q in RELAY else c_copy)(q, 1 - row).wait_recv()

        first = c_bufs[q][:, :, pl.ds(0, NB)].reshape(SIDE * size, NB)
        second = c_bufs[q][:, :, pl.ds(NB, NB)].reshape(SIDE * size, NB)
        panel0 = dot(first, inv[0]).astype(BF16)
        second = (second.astype(F32) - dot(panel0, dt[0])).astype(BF16)
        panel1 = dot(second, inv[1])
        line = lax.broadcasted_iota(jnp.int32, panel1.shape, 0)
        panel1 = jnp.where((line < size) & (r == 0), 0.0, panel1).astype(BF16)
        l_buf[pl.ds(0, SIDE * size), pl.ds(0, NB)] = panel0
        l_buf[pl.ds(0, SIDE * size), pl.ds(NB, NB)] = panel1

        @pl.when(c == 0)
        def _():
            fac_out[:, rows(q), :] = panel0.reshape(SIDE, size, NB)

        @pl.when(c == 1)
        def _():
            fac_out[:, rows(q), :] = panel1.reshape(SIDE, size, NB)

        a_cps[q].wait()

        def tile_step(j, _):
            cols = pl.ds(pl.multiple_of(j * NB, NB), NB)
            both = b_buf[:, :, cols].reshape(2 * NB, NB)
            prod = dot(l_buf[pl.ds(0, SIDE * size), :], both)
            block = a_bufs[q][:, :, cols].astype(F32).reshape(SIDE * size, NB)
            block = (block - prod).astype(BF16).reshape(SIDE, size, NB)
            for i in range(SIDE):
                tiles[i * SIDE + j, pl.ds(0, size), :] = block[i]
            return 0

        lax.fori_loop(0, SIDE, tile_step, 0)

        for s in range(2):
            r_bufs[q][s] = tiles[tab_s[0, 2 * me + s], pl.ds(0, size), :]
        for d in ORDER:
            k = OFFSETS.index(d)
            g = peer(d)
            for s in range(2):
                s_bufs[q][2 * k + s] = tiles[tab_s[0, 2 * g + s], pl.ds(0, size), :]
            if q < HELD and d in ACROSS:

                @pl.when(c == 1)
                def _():
                    x_copy(q, d).start()

            else:
                x_copy(q, d).start()
        if q == 0:
            for d in ORDER:
                pos_copy(d).start()
            for cp in p_cps:
                cp.start()
        if q == 1:
            send_columns([3], [])
        if q == HELD - 1:
            send_columns([HELD + 1], range(2, HELD))
            send_columns([HELD + 2], [HELD])
        elif q >= HELD and q + 3 < NQ:
            send_columns([q + 3], [q + 1])
        if q == min(RELAY) - 1:
            for by in RELAY:
                forward(by)
        if q == HELD - 1:
            @pl.when(c == 0)
            def _():
                for early in range(HELD):
                    for d in ACROSS:
                        x_copy(early, d).start()

    def all_pos():
        some = pl.ds(8, 8 * (GROUPS - 1))
        return pltpu.make_async_remote_copy(
            pos_send.at[some],
            pos_recv.at[some],
            pos_ss,
            pos_rs,
            device_id=(other, r, c),
            device_id_type=MESH,
        )

    def all_x(q):
        some = pl.ds(2, 2 * (GROUPS - 1))
        return pltpu.make_async_remote_copy(
            s_bufs[q].at[some],
            r_bufs[q].at[some],
            x_ss.at[q],
            x_rs.at[q],
            device_id=(other, r, c),
            device_id_type=MESH,
        )

    all_pos().wait_recv()
    got = pos_recv[...]
    lane8 = lax.broadcasted_iota(jnp.int32, (GROUPS * 8, 128), 1)

    def slot_of(v):
        return jnp.where(v >= 0, (v >> 3) * 2 + (v & 1), -1)

    last = jnp.max(jnp.where(got == lane8, sub8, -1), axis=0, keepdims=True)
    got_v[pl.ds(0, 8), :] = jnp.broadcast_to(slot_of(last), (8, 128))
    eye = lax.broadcasted_iota(jnp.int32, (128, 128), 0) == lax.broadcasted_iota(
        jnp.int32, (128, 128), 1
    )
    for h in range(2):
        own = jnp.sum(
            jnp.where(eye, got[h * 128 : (h + 1) * 128], 0), axis=0, keepdims=True
        )
        prev = jnp.max(
            jnp.where((got == own) & (sub8 < lane8 + h * 128), sub8, -1), axis=0, keepdims=True
        )
        prev = jnp.where(own >= 0, prev, -1)
        got_v[pl.ds(8 + 8 * h, 8), :] = jnp.broadcast_to(slot_of(prev), (8, 128))
    got_cp = pltpu.make_async_copy(got_v, got_s, t_sem.at[1])
    got_cp.start()
    got_cp.wait()
    all_pos().wait_send()
    @pl.when((r == 0) & (c == 0))
    def _():
        for i in range(2):
            dt_copy(i).wait_send()

    @pl.when((r == 0) & (c == 1))
    def _():
        for i in range(2):
            dt_pass(i).wait_send()

    @pl.when(r == 0)
    def _():
        b_copy.wait_send()

    for row in range(2):

        @pl.when((r == row) & (c == 0))
        def _():
            for q in range(NQ):
                if q not in left:
                    c_copy(q, 1 - row).wait_send()

        @pl.when((r == row) & (c == 1))
        def _():
            for q in RELAY:
                by_copy(q, 1 - row).wait_send()

    for q in range(NQ):
        if q == NQ - 1:
            for sent in range(NQ - 1):
                all_x(sent).wait_send()
            p_cps[q].wait()
        all_x(q).wait_recv()
        if q < NQ - 1:
            chain(got_s, r_bufs[q], acc, CHUNKS[q])
            p_cps[q].wait()
            place_all(got_s, acc, out.at[:, rows(q), :], out.at[:, rows(q), :], CHUNKS[q])
    all_x(NQ - 1).wait_send()


def finish(factor, part, arrived, got, fac_out, out, got_s, acc, rest, sem):
    done = STARTS[-1]
    got_cp = pltpu.make_async_copy(got, got_s, sem.at[0])
    got_cp.start()
    moves = [pltpu.make_async_copy(factor, fac_out, sem.at[1])]
    for i in range(SIDE):
        ready = pl.ds(0, done)
        moves.append(
            pltpu.make_async_copy(part.at[i, ready, :], out.at[i, ready, :], sem.at[3 + i])
        )
    for cp in moves:
        cp.start()
    got_cp.wait()
    chain(got_s, arrived, acc, LAST)
    place_all(got_s, acc, part.at[:, pl.ds(done, LAST), :], rest, LAST)
    last_cp = pltpu.make_async_copy(rest, out.at[:, pl.ds(done, LAST), :], sem.at[2])
    last_cp.start()
    for cp in moves + [last_cp]:
        cp.wait()


def body(front, inverses, routes, positions, parent):
    hbm = pl.BlockSpec(memory_space=pl.ANY)
    smem = pl.BlockSpec(memory_space=pltpu.SMEM)
    vmem = pl.BlockSpec(memory_space=pltpu.VMEM)
    most = max(CHUNKS)
    dma = pltpu.SemaphoreType.DMA

    def per_chunk(shape, chunks=CHUNKS):
        return [pltpu.VMEM(shape(n), BF16) for n in chunks]

    scratch = (
        per_chunk(lambda n: (SIDE, n, 2 * NB))
        + per_chunk(lambda n: (SIDE, n, WIDTH))
        + per_chunk(lambda n: (TILES, n, NB))
        + per_chunk(lambda n: (TILES, n, NB), CHUNKS[:-1])
        + per_chunk(lambda n: (SIDE, n, 2 * NB), [CHUNKS[q] for q in RELAY])
        + [
            pltpu.VMEM((2, NB, WIDTH), BF16),
            pltpu.VMEM((2, NB, NB), BF16),
            pltpu.VMEM((SIDE * most, 2 * NB), BF16),
            pltpu.VMEM((TILES, most, NB), BF16),
            pltpu.VMEM((TILES, most, NB), F32),
            pltpu.VMEM((GROUPS * 8, 128), jnp.int32),
            pltpu.VMEM((GROUPS * 8, 128), jnp.int32),
            pltpu.VMEM((8, 128), jnp.int32),
            pltpu.SMEM((8, 128), jnp.int32),
            pltpu.SMEM((24, 128), jnp.int32),
        ]
        + [dma((NQ,))] * 6
        + [dma, dma]
        + [dma, dma, dma((2,)), dma((2,)), dma((2,)), dma((NQ,)), dma((NQ,))]
    )
    factor, part, arrived, got = pl.pallas_call(
        kernel,
        out_shape=(
            pltpu.VMEM((SIDE, NB, NB), BF16),
            pltpu.VMEM((SIDE, NB, WIDTH), BF16),
            pltpu.VMEM((TILES, LAST, NB), BF16),
            pltpu.VMEM((24, 128), jnp.int32),
        ),
        in_specs=[hbm, vmem, smem, smem, hbm],
        out_specs=(vmem,) * 4,
        scratch_shapes=scratch,
        compiler_params=pltpu.CompilerParams(
            collective_id=0, has_side_effects=True, vmem_limit_bytes=50 * 2**20
        ),
        cost_estimate=pl.CostEstimate(
            flops=2 * WIDTH * WIDTH * 2 * NB, bytes_accessed=25 * 2**20, transcendentals=0
        ),
        name="eliminate_exchange_add",
    )(
        front.reshape(SIDE, NB, WIDTH),
        inverses[0],
        routes[0],
        positions[0],
        parent.reshape(SIDE, NB, WIDTH),
    )
    factor, added = pl.pallas_call(
        finish,
        out_shape=(
            jax.ShapeDtypeStruct((SIDE, NB, NB), BF16),
            jax.ShapeDtypeStruct((SIDE, NB, WIDTH), BF16),
        ),
        in_specs=[vmem] * 4,
        out_specs=(hbm, hbm),
        scratch_shapes=[
            pltpu.SMEM((24, 128), jnp.int32),
            pltpu.VMEM((TILES, LAST, NB), F32),
            pltpu.VMEM((SIDE, LAST, WIDTH), BF16),
            dma((3 + SIDE,)),
        ],
        compiler_params=pltpu.CompilerParams(vmem_limit_bytes=30 * 2**20),
        cost_estimate=pl.CostEstimate(
            flops=2 * TILES * LAST * NB, bytes_accessed=10 * 2**20, transcendentals=0
        ),
        name="finish",
    )(factor, part, arrived, got)
    return factor.reshape(1, WIDTH, NB), added.reshape(1, WIDTH, WIDTH)


def solution(mesh):
    return jax.shard_map(
        body,
        mesh=mesh,
        in_specs=(
            P("front", "row", "col"),
            P("front", None, None, None),
            P("front", "row", "col"),
            P("front", "row", "col"),
            P("front", "row", "col"),
        ),
        out_specs=(P("front", "row", "col"), P("front", "row", "col")),
        check_vma=False,
    )
```
